32 devices in a mesh: groups: 2 (over x), tensor: 16 (over z, y, core).
Axes of the slice: x: 2, y: 2, z: 4, core: 2. Of those that a mesh axis runs over, the one named last changes fastest.
Arguments:
- queries: bfloat16 [1024, 2048], P('groups', 'tensor'), parts along dimension 0, may hold values from -600 to 600
- block_key_rows: bfloat16 [1024, 2048], P('groups', 'tensor'), parts along dimension 0, may hold values from -5 to 5
- block_value_rows: bfloat16 [1024, 2048], P('groups', 'tensor'), parts along dimension 0, may hold values from -6 to 6
- cached_key_rows: bfloat16 [24576, 2048], P('groups', 'tensor'), parts along dimension 0, may hold values from -6 to 6
- cached_value_rows: bfloat16 [24576, 2048], P('groups', 'tensor'), parts along dimension 0, may hold values from -6 to 6
- output_projection_weight: bfloat16 [2048, 5120], P('tensor'), may hold values from -0.125 to 0.125
- stored_shrink_matrices: bfloat16 [32, 2048, 64], P('tensor'), may hold values from -0.125 to 0.125
- stored_expand_matrices: bfloat16 [32, 64, 5120], P('tensor'), may hold values from -0.75 to 0.75
- request_adapter_index: int32 [16], P('groups'), parts along dimension 0, may hold values from 0 to 31
- adapter_storage_row: int32 [32], replicated, may hold values from 0 to 31, each once
- block_token_lengths: int32 [16], P('groups'), parts along dimension 0, may hold values from 1 to 256, 512 in all
- cached_token_lengths: int32 [16], P('groups'), parts along dimension 0, may hold values from 1 to 6144, 12288 in all
Outputs:
- mixed: bfloat16 [1024, 5120], P(('groups', 'tensor')), parts along dimension 0
The draws below stay inside these ranges and needn't reach their ends.
There are 2 independent parts, one for each index of `groups`. The reference program is written for one: setup_inputs(seed, part) draws one part's arguments, and reference() takes and returns one part's arrays. A program takes and returns all parts, laid end to end along the dimension named above; an argument that names none is the same for every part. Nothing has to cross between parts.
Inputs may be any that keep to these rules, and one draw needn't show every extreme that they name: `adapter_storage_row`: each adapter's row in stored_shrink_matrices and stored_expand_matrices; every row once. `block_token_lengths`: sum to 512. `cached_token_lengths`: sum to 12288.
All inputs are finite; a program needn't handle non-finite values.
Results may differ from the reference program's by a relative error of at most 0.0058.
Values may be sent and summed in bfloat16 or wider, within the bound.
A program may use at most 128 MiB of HBM per device.

```python
import math
import jax
import jax.numpy as jnp
import numpy as np
from jax import lax

MODEL_SIZE = 5120
HD = 128
ADAPTER_RANK = 64
TOK = 512
CTX = 12288
REQ = 8
HEADS = 16
QUERY_WIDTH = 2048
ADAPTER_TOTAL = 32
KEYS = 12800


def shared_draw(key):
    base_keys = jax.random.truncated_normal(key, -4.0, 4.0, (TOK, QUERY_WIDTH), jnp.float32)
    return base_keys


def draw_block_key_rows(key, part):
    base_keys = shared_draw(key)
    return base_keys.astype(jnp.bfloat16)


def draw_queries(key, part):
    key = jax.random.fold_in(key, 5)
    return (2.5 * jax.random.truncated_normal(key, -4.0, 4.0, (TOK, QUERY_WIDTH), jnp.float32)).astype(jnp.bfloat16)


def place_ends(drawn, rng, least, top_value):
    shape = drawn.shape
    index_at = [jax.random.randint(jax.random.fold_in(rng, axis), (), 0, shape[axis]) for axis in range(len(shape))]
    drawn = drawn.at[tuple(index_at)].set(least)
    longest = shape.index(max(shape))
    index_at[longest] = (index_at[longest] + 1) % shape[longest]
    return drawn.at[tuple(index_at)].set(top_value)


def block_levels(key, extent, pieces, low, high):
    loudness, own = 1.0, jax.random.fold_in(key, 6)
    for axis_at, shards_of in pieces:
        steps = jnp.exp(jax.random.uniform(jax.random.fold_in(own, axis_at), (shards_of,), jnp.float32, low / len(pieces), high / len(pieces)))
        loudness = loudness * jnp.repeat(steps, extent[axis_at] // shards_of).reshape([-1 if axis == axis_at else 1 for axis in range(len(extent))])
    return loudness


def rank_table(number_of, lean):
    weights = [(1 << 20) // math.isqrt(standing ** lean) + 1 for standing in range(1, number_of + 1)]
    spread = 1 + sum(weights) // (1 << 30)
    return np.cumsum(np.array([max(1, weight // spread) for weight in weights]))


def ranked_ids(stream_key, shape, count, lean):
    table = rank_table(count, lean)
    ticket = jax.random.randint(jax.random.fold_in(stream_key, 1), shape, 0, int(table[count - 1]))
    grade = jnp.searchsorted(jnp.asarray(table, jnp.int32), ticket, side="right")
    return jax.random.permutation(jax.random.fold_in(stream_key, 2), count)[grade].astype(jnp.int32)


def length_profile(amount, total, most, slope):
    portions = [(1 << 20) // math.isqrt(rank ** slope) + 1 for rank in range(2, amount + 1)]
    spare, holding = total - most - (amount - 1), [1] * (amount - 1)
    while spare > 0:
        free = [i for i in range(amount - 1) if holding[i] < most]
        whole, left = sum([portions[i] for i in free]), spare
        for i in free:
            extra = min(most - holding[i], max(1, left * portions[i] // whole), spare)
            holding[i] = holding[i] + extra
            spare = spare - extra
    return np.array([most] + holding)


def ragged(rng, count, total, limit, slope):
    if count == 2:
        one = jax.random.randint(rng, (), max(1, total - limit), min(limit, total - 1) + 1)
        return jnp.stack([one, total - one])
    sizes = jnp.asarray(length_profile(count, total, limit, slope), jnp.int32)
    couples = (count - 1) // 2
    source_of, taker = sizes[1:1 + 2 * couples:2], sizes[2:2 + 2 * couples:2]
    margin = jnp.minimum(source_of - 1, limit - taker)
    passed = jax.random.randint(jax.random.fold_in(rng, 1), (couples,), 0, 1 << 20) % (margin + 1)
    sizes = sizes.at[1:1 + 2 * couples:2].set(source_of - passed).at[2:2 + 2 * couples:2].set(taker + passed)
    return sizes[jax.random.permutation(jax.random.fold_in(rng, 2), count)]


def bell_draw(key, extent, scale, bound, pieces=(), kind=jnp.bfloat16):
    array = scale * jax.random.normal(key, extent, jnp.float32)
    if pieces:
        array = array * block_levels(key, extent, pieces, -0.22, 0.18)
    return jnp.clip(array, -bound, bound).astype(kind)


def setup_inputs(seed: int = 0, part: int = 0) -> dict:
    key_list = jax.random.split(jax.random.key(seed), 13)
    part_splits = jax.random.split(jax.random.fold_in(key_list[12], part), 13)
    return {
        "queries": draw_queries(jax.random.fold_in(jax.random.fold_in(key_list[12], part), 71), part),
        "block_key_rows": draw_block_key_rows(jax.random.fold_in(jax.random.fold_in(key_list[12], part), 71), part),
        "block_value_rows": bell_draw(part_splits[2], (TOK, QUERY_WIDTH), 1.0, 6.0, ((1, 16),)),
        "cached_key_rows": bell_draw(part_splits[3], (CTX, QUERY_WIDTH), 1.0, 6.0, ((1, 16),)),
        "cached_value_rows": bell_draw(part_splits[4], (CTX, QUERY_WIDTH), 1.0, 6.0, ((1, 16),)),
        "output_projection_weight": bell_draw(key_list[5], (QUERY_WIDTH, MODEL_SIZE), QUERY_WIDTH ** -0.5, 0.125, ((0, 16),)),
        "stored_shrink_matrices": bell_draw(key_list[6], (ADAPTER_TOTAL, QUERY_WIDTH, ADAPTER_RANK), QUERY_WIDTH ** -0.5, 0.125, ((0, 16),)),
        "stored_expand_matrices": bell_draw(key_list[7], (ADAPTER_TOTAL, ADAPTER_RANK, MODEL_SIZE), ADAPTER_RANK ** -0.5, 0.75, ((0, 16),)),
        "request_adapter_index": place_ends(ranked_ids(part_splits[8], (REQ,), ADAPTER_TOTAL, 2), jax.random.fold_in(part_splits[8], 3), 0, ADAPTER_TOTAL - 1).astype(jnp.int32),
        "adapter_storage_row": jax.random.permutation(key_list[9], ADAPTER_TOTAL).astype(jnp.int32),
        "block_token_lengths": ragged(part_splits[10], REQ, TOK, TOK // 2, 2).astype(jnp.int32),
        "cached_token_lengths": ragged(part_splits[11], REQ, CTX, CTX // 2, 2).astype(jnp.int32),
    }


def request_ids(lengths, total):
    segment_ends = jnp.cumsum(lengths)
    positions = jnp.arange(total, dtype=jnp.int32)
    return jnp.sum((positions[:, None] >= segment_ends[None, :]).astype(jnp.int32), axis=1)


def reference(queries, block_key_rows, block_value_rows, cached_key_rows, cached_value_rows, output_projection_weight, stored_shrink_matrices, stored_expand_matrices, request_adapter_index, adapter_storage_row, block_token_lengths, cached_token_lengths):
    token_req = request_ids(block_token_lengths, TOK)
    cache_req = request_ids(cached_token_lengths, CTX)
    key_req = jnp.concatenate([cache_req, token_req])
    token_pos = jnp.arange(TOK, dtype=jnp.int32)
    key_pos = jnp.concatenate([jnp.full((CTX,), -1, jnp.int32), token_pos])
    visible = (key_req[None, :] == token_req[:, None]) & (key_pos[None, :] <= token_pos[:, None])
    all_keys = jnp.concatenate([cached_key_rows, block_key_rows], axis=0)
    all_values = jnp.concatenate([cached_value_rows, block_value_rows], axis=0)
    query_heads = queries.reshape(TOK, HEADS, HD).transpose(1, 0, 2)
    key_heads = all_keys.reshape(KEYS, HEADS, HD).transpose(1, 0, 2)
    value_heads = all_values.reshape(KEYS, HEADS, HD).transpose(1, 0, 2)
    score_scale = HD ** -0.5

    def one_head(operands):
        head_q, head_k, head_v = operands
        scores = jnp.dot(head_q, head_k.T, preferred_element_type=jnp.float32) * score_scale
        scores = jnp.where(visible, scores, -jnp.inf)
        weights = jax.nn.softmax(scores, axis=1).astype(jnp.bfloat16)
        return jnp.dot(weights, head_v, preferred_element_type=jnp.float32).astype(jnp.bfloat16)

    attended = lax.map(one_head, (query_heads, key_heads, value_heads))
    attended = attended.transpose(1, 0, 2).reshape(TOK, QUERY_WIDTH)
    adapter_row_ids = adapter_storage_row[request_adapter_index]
    shrink_matrix_list = stored_shrink_matrices[adapter_row_ids]
    expand_matrix_list = stored_expand_matrices[adapter_row_ids]
    shrink_flattened = shrink_matrix_list.transpose(1, 0, 2).reshape(QUERY_WIDTH, REQ * ADAPTER_RANK)
    shrink_every_token = jnp.dot(attended, shrink_flattened, preferred_element_type=jnp.float32).reshape(TOK, REQ, ADAPTER_RANK)
    onehot = (token_req[:, None] == jnp.arange(REQ, dtype=jnp.int32)[None, :]).astype(jnp.float32)
    shrunk = jnp.sum(shrink_every_token * onehot[:, :, None], axis=1)
    expanded = (onehot[:, :, None] * shrunk[:, None, :]).reshape(TOK, REQ * ADAPTER_RANK)
    delta = jnp.dot(expanded, expand_matrix_list.reshape(REQ * ADAPTER_RANK, MODEL_SIZE).astype(jnp.float32), precision=lax.Precision.HIGHEST)
    base_out = jnp.dot(attended, output_projection_weight, preferred_element_type=jnp.float32)
    return (base_out + delta).astype(jnp.bfloat16)
```

```python
import functools
import math

import jax
import jax.numpy as jnp
from jax import lax
from jax.experimental import pallas as pl
from jax.experimental.pallas import tpu as pltpu
from jax.sharding import PartitionSpec as P

HD = 128
SUB = 4
BIG = 2.0**40
F32 = jnp.float32
BF16 = jnp.bfloat16


def dot_nt(a, b):
    return lax.dot_general(a, b, (((1,), (1,)), ((), ())), preferred_element_type=F32)


def pick(position, bounds, values, like):
    out = like
    for r, value in enumerate(values):
        inside = (position >= bounds[r]) & (position < bounds[r + 1])
        out = jnp.where(inside, value, out)
    return out


def kernel(
    n,
    q_chunk,
    key_block,
    q_hbm,
    bk_hbm,
    bv_hbm,
    ck_hbm,
    cv_hbm,
    w_hbm,
    s_hbm,
    e_hbm,
    req_adapter,
    storage_row,
    block_len,
    cache_len,
    out_ref,
    q2,
    k2,
    v2,
    w_all,
    e_all,
    s_all,
    att_all,
    shr_part,
    shr_recv,
    shr_full,
    part,
    recv,
    base,
    load_sem,
    w_send,
    w_recv,
    e_send,
    e_recv,
    s_send,
    s_recv,
    a_send,
    a_recv,
    p_send,
    p_recv,
    f_send,
    f_recv,
    o_send,
    o_recv,
):
    t = lax.axis_index("tensor")
    j = lax.rem(t, SUB)
    first = t - j
    tokens = q_hbm.shape[0]
    cached = ck_hbm.shape[0]
    requests = block_len.shape[0]
    rows = tokens // n
    width = w_hbm.shape[1] // SUB
    own_adapters = s_hbm.shape[0]
    chunks = tokens // q_chunk
    per_chunk = n // chunks

    loads = [
        pltpu.make_async_copy(q_hbm, q2.at[:, pl.ds(0, HD)], load_sem.at[0]),
        pltpu.make_async_copy(bk_hbm, k2.at[pl.ds(0, tokens), pl.ds(0, HD)], load_sem.at[1]),
        pltpu.make_async_copy(ck_hbm, k2.at[pl.ds(tokens, cached), pl.ds(0, HD)], load_sem.at[2]),
        pltpu.make_async_copy(bv_hbm, v2.at[pl.ds(0, tokens), pl.ds(0, HD)], load_sem.at[3]),
        pltpu.make_async_copy(cv_hbm, v2.at[pl.ds(tokens, cached), pl.ds(0, HD)], load_sem.at[4]),
    ]
    for load in loads:
        load.start()

    def columns(block):
        return pl.ds(pl.multiple_of(block * width, 128), width)

    def heads_columns(device):
        return pl.ds(pl.multiple_of(device * HD, HD), HD)

    own_loads = [
        pltpu.make_async_copy(w_hbm.at[:, columns(j)], w_all.at[j], load_sem.at[5]),
        pltpu.make_async_copy(e_hbm.at[:, columns(j)], e_all.at[j], load_sem.at[6]),
        pltpu.make_async_copy(s_hbm.at[:, :, heads_columns(t)], s_all.at[t], load_sem.at[7]),
    ]
    for load in own_loads:
        load.start()

    barrier = pltpu.get_barrier_semaphore()
    for k in range(1, n):
        pl.semaphore_signal(
            barrier,
            inc=1,
            device_id={"tensor": lax.rem(t + k, n)},
            device_id_type=pl.DeviceIdType.MESH,
        )
    pl.semaphore_wait(barrier, n - 1)

    def remote(src, dst, send_sem, recv_sem, device):
        return pltpu.make_async_remote_copy(
            src_ref=src,
            dst_ref=dst,
            send_sem=send_sem,
            recv_sem=recv_sem,
            device_id={"tensor": device},
            device_id_type=pl.DeviceIdType.MESH,
        )

    def shrink_copy(k, sender, device):
        return remote(
            s_hbm.at[:, :, heads_columns(device)], s_all.at[sender], s_send.at[k], s_recv.at[k], device
        )

    def weight_copy(k, sender_j, jj):
        return remote(
            w_hbm.at[:, columns(jj)], w_all.at[sender_j], w_send.at[k], w_recv.at[k], first + jj
        )

    def expand_copy(k, sender_j, jj):
        return remote(
            e_hbm.at[:, columns(jj)], e_all.at[sender_j], e_send.at[k], e_recv.at[k], first + jj
        )

    for k in range(1, n):
        shrink_copy(k, t, lax.rem(t + k, n)).start()
    for k in range(1, SUB):
        weight_copy(k, j, lax.rem(j + k, SUB)).start()
    for k in range(1, SUB):
        expand_copy(k, j, lax.rem(j + k, SUB)).start()

    token_bounds, cache_bounds, adapter_rows = [jnp.int32(0)], [jnp.int32(0)], []
    for r in range(requests):
        token_bounds.append(token_bounds[r] + block_len[r])
        cache_bounds.append(cache_bounds[r] + cache_len[r])
        adapter_rows.append(storage_row[req_adapter[r]])

    lane1 = lax.broadcasted_iota(jnp.int32, (1, HD), 1)
    token_lo = jnp.zeros((1, HD), jnp.int32)
    token_hi = jnp.zeros((1, HD), jnp.int32)
    cache_lo = jnp.zeros((1, HD), jnp.int32)
    cache_hi = jnp.zeros((1, HD), jnp.int32)
    for r in range(requests):
        token_lo = jnp.where(lane1 == r, token_bounds[r], token_lo)
        token_hi = jnp.where(lane1 == r, token_bounds[r + 1], token_hi)
        cache_lo = jnp.where(lane1 == r, cache_bounds[r], cache_lo)
        cache_hi = jnp.where(lane1 == r, cache_bounds[r + 1], cache_hi)
    token_pos = lax.broadcasted_iota(jnp.int32, (tokens, HD), 0)
    token_in = (token_pos >= token_lo) & (token_pos < token_hi)
    q2[:, HD:] = jnp.where(token_in, 0.0, -BIG).astype(BF16)
    k2[0:tokens, HD:] = jnp.where(token_in, 1.0, 0.0).astype(BF16)
    ones = jnp.ones((tokens, HD), BF16)
    v2[0:tokens, HD:] = ones

    def augment(i, carry):
        at = pl.multiple_of(tokens + i * tokens, tokens)
        pos = token_pos + i * tokens
        inside = (pos >= cache_lo) & (pos < cache_hi)
        k2[pl.ds(at, tokens), HD:] = jnp.where(inside, 1.0, 0.0).astype(BF16)
        v2[pl.ds(at, tokens), HD:] = ones
        return carry

    lax.fori_loop(0, cached // tokens, augment, 0)
    for load in loads:
        load.wait()
    for load in own_loads:
        load.wait()

    scale = HD**-0.5 * math.log2(math.e)
    adapters = n * own_adapters

    def att_copy(c, k, sender_j, jj):
        span = pl.ds(c * q_chunk, q_chunk)
        return remote(
            att_all.at[sender_j, span],
            att_all.at[sender_j, span],
            a_send.at[c, k],
            a_recv.at[c, k],
            first + jj,
        )

    def row_slice(ref, device):
        return ref.at[pl.ds(pl.multiple_of(device * rows, rows), rows)]

    def shr_copy(sender, device):
        return remote(
            row_slice(shr_part, device),
            shr_recv.at[sender],
            p_send.at[device],
            p_recv.at[sender],
            device,
        )

    for c in range(chunks):
        q = q2[pl.ds(c * q_chunk, q_chunk), :]
        scores = dot_nt(q, k2[0:tokens, :])
        row = lax.broadcasted_iota(jnp.int32, scores.shape, 0) + c * q_chunk
        col = lax.broadcasted_iota(jnp.int32, scores.shape, 1)
        scores = jnp.where(col <= row, scores, -BIG)
        top = jnp.max(scores, axis=1, keepdims=True)
        p = jnp.exp2((scores - top) * scale).astype(BF16)
        acc = jnp.dot(p, v2[0:tokens, :], preferred_element_type=F32)

        def step(i, carry):
            top, acc = carry
            at = pl.multiple_of(tokens + i * key_block, 512)
            scores = dot_nt(q, k2[pl.ds(at, key_block), :])
            new_top = jnp.maximum(top, jnp.max(scores, axis=1, keepdims=True))
            p = jnp.exp2((scores - new_top) * scale).astype(BF16)
            acc = acc * jnp.exp2((top - new_top) * scale)
            return new_top, acc + jnp.dot(p, v2[pl.ds(at, key_block), :], preferred_element_type=F32)

        top, acc = lax.fori_loop(0, cached // key_block, step, (top, acc))
        attended = (acc[:, :HD] / acc[:, HD:]).astype(BF16)
        span = pl.ds(c * q_chunk, q_chunk)
        att_all[j, span] = attended
        for k in range(1, SUB):
            att_copy(c, k, j, lax.rem(j + k, SUB)).start()

        if c == 0:
            for k in range(1, n):
                shrink_copy(k, lax.rem(t + n - k, n), t).wait_recv()
        pos = lax.broadcasted_iota(jnp.int32, (q_chunk, HD), 0) + c * q_chunk
        lane = lax.broadcasted_iota(jnp.int32, (q_chunk, HD), 1)
        token_row = pick(pos, token_bounds, adapter_rows, jnp.zeros((q_chunk, HD), jnp.int32))
        half = jnp.where(lane >= HD // 2, 1, 0)
        shr = jnp.zeros((q_chunk, HD), F32)
        for a in range(0, adapters, 2):
            matrices = s_all[a // own_adapters].reshape(HD, HD)
            product = dot_nt(attended, matrices)
            shr = jnp.where(token_row == half + a, product, shr)
        shr_part[span, :] = shr + pltpu.roll(shr, HD // 2, 1)
        for k in range(per_chunk):
            device = c * per_chunk + lax.rem(t + k, per_chunk)

            @pl.when(device != t)
            def _():
                shr_copy(t, device).start()

    total = row_slice(shr_part, t)[...]
    for k in range(1, n):
        sender = lax.rem(t + n - k, n)
        shr_copy_in = remote(
            row_slice(shr_part, t), shr_recv.at[sender], p_send.at[sender], p_recv.at[sender], sender
        )
        shr_copy_in.wait_recv()
        total = total + shr_recv[sender]
    row_slice(shr_full, t)[...] = total

    def full_copy(k, sender, device):
        return remote(
            row_slice(shr_full, sender), row_slice(shr_full, sender), f_send.at[k], f_recv.at[k], device
        )

    for k in range(1, n):
        full_copy(k, t, lax.rem(t + k, n)).start()

    for k in range(1, SUB):
        source = lax.rem(j + SUB - k, SUB)
        weight_copy(k, source, j).wait_recv()
        for c in range(chunks):
            att_copy(c, k, source, j).wait_recv()
    for c in range(chunks):
        span = pl.ds(c * q_chunk, q_chunk)
        value = jnp.dot(att_all[0, span], w_all[0], preferred_element_type=F32)
        for s in range(1, SUB):
            value = value + jnp.dot(att_all[s, span], w_all[s], preferred_element_type=F32)
        base[span, :] = value

    for k in range(1, SUB):
        expand_copy(k, lax.rem(j + SUB - k, SUB), j).wait_recv()
    for k in range(1, n):
        full_copy(k, lax.rem(t + n - k, n), t).wait_recv()

    def part_copy(sender, device):
        return remote(part.at[device], recv.at[sender], o_send.at[device], o_recv.at[sender], device)

    for c in range(chunks):
        span = pl.ds(c * q_chunk, q_chunk)
        pos = lax.broadcasted_iota(jnp.int32, (q_chunk, HD), 0) + c * q_chunk
        lane = lax.broadcasted_iota(jnp.int32, (q_chunk, HD), 1)
        token_row = pick(pos, token_bounds, adapter_rows, jnp.zeros((q_chunk, HD), jnp.int32))
        half = jnp.where(lane >= HD // 2, 1, 0)
        shrunk = shr_full[span, :]
        value = base[span, :]
        for s in range(SUB):
            mine = jnp.where(token_row == half + (first + s) * own_adapters, shrunk, 0.0)
            high = mine.astype(BF16)
            low = (mine - high.astype(F32)).astype(BF16)
            value = value + jnp.dot(high, e_all[s], preferred_element_type=F32)
            value = value + jnp.dot(low, e_all[s], preferred_element_type=F32)
        per = value.astype(part.dtype).reshape(per_chunk, rows, width)
        part[pl.ds(c * per_chunk, per_chunk)] = per
        for k in range(per_chunk):
            device = c * per_chunk + lax.rem(t + k, per_chunk)

            @pl.when(device != t)
            def _():
                part_copy(t, device).start()

    recv[t] = part[t]
    for k in range(1, n):
        sender = lax.rem(t + n - k, n)
        part_in = remote(part.at[sender], recv.at[sender], o_send.at[sender], o_recv.at[sender], sender)
        part_in.wait_recv()
    for s in range(SUB):
        value = recv[s].astype(F32)
        for z in range(1, n // SUB):
            value = value + recv[z * SUB + s].astype(F32)
        out_ref[:, s * width : (s + 1) * width] = value.astype(out_ref.dtype)

    for k in range(1, n):
        device = lax.rem(t + k, n)
        shrink_copy(k, t, device).wait_send()
        full_copy(k, t, device).wait_send()
        shr_copy(t, device).wait_send()
        part_copy(t, device).wait_send()
    for k in range(1, SUB):
        jj = lax.rem(j + k, SUB)
        weight_copy(k, j, jj).wait_send()
        expand_copy(k, j, jj).wait_send()
        for c in range(chunks):
            att_copy(c, k, j, jj).wait_send()


def on_device(
    queries,
    block_key_rows,
    block_value_rows,
    cached_key_rows,
    cached_value_rows,
    output_projection_weight,
    stored_shrink_matrices,
    stored_expand_matrices,
    request_adapter_index,
    adapter_storage_row,
    block_token_lengths,
    cached_token_lengths,
):
    n = lax.axis_size("tensor")
    tokens = queries.shape[0]
    cached = cached_key_rows.shape[0]
    model = output_projection_weight.shape[1]
    own, _, rank = stored_shrink_matrices.shape
    rows = tokens // n
    width = model // SUB
    q_chunk = 256
    key_block = 1536
    chunks = tokens // q_chunk
    send_type = BF16 if rows % 16 == 0 else F32
    shrink_t = stored_shrink_matrices.transpose(0, 2, 1)
    expand = stored_expand_matrices.reshape(own * rank, model)
    hbm = pl.BlockSpec(memory_space=pl.ANY)
    smem = pl.BlockSpec(memory_space=pltpu.SMEM)
    dma = pltpu.SemaphoreType.DMA
    return pl.pallas_call(
        functools.partial(kernel, n, q_chunk, key_block),
        out_shape=jax.ShapeDtypeStruct((rows, model), BF16),
        in_specs=[hbm] * 8 + [smem] * 4,
        out_specs=pl.BlockSpec(memory_space=pltpu.VMEM),
        scratch_shapes=[
            pltpu.VMEM((tokens, 2 * HD), BF16),
            pltpu.VMEM((tokens + cached, 2 * HD), BF16),
            pltpu.VMEM((tokens + cached, 2 * HD), BF16),
            pltpu.VMEM((SUB, HD, width), BF16),
            pltpu.VMEM((SUB, own * rank, width), BF16),
            pltpu.VMEM((n, own, rank, HD), BF16),
            pltpu.VMEM((SUB, tokens, HD), BF16),
            pltpu.VMEM((tokens, HD), F32),
            pltpu.VMEM((n, rows, HD), F32),
            pltpu.VMEM((tokens, HD), F32),
            pltpu.VMEM((n, rows, width), send_type),
            pltpu.VMEM((n, rows, width), send_type),
            pltpu.VMEM((tokens, width), F32),
            dma((8,)),
            dma((SUB,)),
            dma((SUB,)),
            dma((SUB,)),
            dma((SUB,)),
            dma((n,)),
            dma((n,)),
            dma((chunks, SUB)),
            dma((chunks, SUB)),
            dma((n,)),
            dma((n,)),
            dma((n,)),
            dma((n,)),
            dma((n,)),
            dma((n,)),
        ],
        compiler_params=pltpu.CompilerParams(
            collective_id=0, has_side_effects=True, vmem_limit_bytes=56 * 1024 * 1024
        ),
    )(
        queries,
        block_key_rows,
        block_value_rows,
        cached_key_rows,
        cached_value_rows,
        output_projection_weight,
        shrink_t,
        expand,
        request_adapter_index,
        adapter_storage_row,
        block_token_lengths,
        cached_token_lengths,
    )


def solution(mesh):
    placed = (
        P("groups", "tensor"),
        P("groups", "tensor"),
        P("groups", "tensor"),
        P("groups", "tensor"),
        P("groups", "tensor"),
        P("tensor", None),
        P("tensor", None, None),
        P("tensor", None, None),
        P("groups"),
        P(),
        P("groups"),
        P("groups"),
    )
    return jax.shard_map(
        on_device,
        mesh=mesh,
        in_specs=placed,
        out_specs=P(("groups", "tensor"), None),
        check_vma=False,
    )
```

```python
import functools
import math

import jax
import jax.numpy as jnp
from jax import lax
from jax.experimental import pallas as pl
from jax.experimental.pallas import tpu as pltpu
from jax.sharding import PartitionSpec as P

HD = 128
SUB = 8
BIG = 2.0**40
F32 = jnp.float32
BF16 = jnp.bfloat16


def dot_nt(a, b):
    return lax.dot_general(a, b, (((1,), (1,)), ((), ())), preferred_element_type=F32)


def pick(position, bounds, values, like):
    out = like
    for r, value in enumerate(values):
        inside = (position >= bounds[r]) & (position < bounds[r + 1])
        out = jnp.where(inside, value, out)
    return out


def pack(twice, kind):
    high = twice.astype(BF16).astype(F32)
    lane = lax.broadcasted_iota(jnp.int32, twice.shape, 1)
    return jnp.where(lane < HD // 2, high, twice - high).astype(kind)


def unpack(packed):
    halves = packed.astype(F32)
    return halves + pltpu.roll(halves, HD // 2, 1)


def kernel(
    n,
    q_chunk,
    key_block,
    q_hbm,
    bk_hbm,
    bv_hbm,
    ck_hbm,
    cv_hbm,
    w_hbm,
    s_hbm,
    e_hbm,
    req_adapter,
    storage_row,
    block_len,
    cache_len,
    out_ref,
    q2,
    k2,
    v2,
    w_all,
    e_all,
    s_all,
    att_all,
    shr_part,
    shr_recv,
    shr_full,
    part,
    recv,
    base,
    load_sem,
    w_send,
    w_recv,
    e_send,
    e_recv,
    s_send,
    s_recv,
    a_send,
    a_recv,
    p_send,
    p_recv,
    f_send,
    f_recv,
    o_send,
    o_recv,
):
    t = lax.axis_index("tensor")
    j = lax.rem(t, SUB)
    first = t - j
    tokens = q_hbm.shape[0]
    cached = ck_hbm.shape[0]
    requests = block_len.shape[0]
    rows = tokens // n
    width = w_hbm.shape[1] // SUB
    own_adapters = s_hbm.shape[0]
    chunks = tokens // q_chunk
    per_chunk = n // chunks

    loads = [
        pltpu.make_async_copy(q_hbm, q2.at[:, pl.ds(0, HD)], load_sem.at[0]),
        pltpu.make_async_copy(bk_hbm, k2.at[pl.ds(0, tokens), pl.ds(0, HD)], load_sem.at[1]),
        pltpu.make_async_copy(ck_hbm, k2.at[pl.ds(tokens, cached), pl.ds(0, HD)], load_sem.at[2]),
        pltpu.make_async_copy(bv_hbm, v2.at[pl.ds(0, tokens), pl.ds(0, HD)], load_sem.at[3]),
        pltpu.make_async_copy(cv_hbm, v2.at[pl.ds(tokens, cached), pl.ds(0, HD)], load_sem.at[4]),
    ]
    for load in loads:
        load.start()

    def columns(block):
        return pl.ds(pl.multiple_of(block * width, 128), width)

    def heads_columns(device):
        return pl.ds(pl.multiple_of(device * HD, HD), HD)

    own_loads = [
        pltpu.make_async_copy(w_hbm.at[:, columns(j)], w_all.at[j], load_sem.at[5]),
        pltpu.make_async_copy(e_hbm.at[:, columns(j)], e_all.at[j], load_sem.at[6]),
        pltpu.make_async_copy(s_hbm.at[:, :, heads_columns(t)], s_all.at[t], load_sem.at[7]),
    ]
    for load in own_loads:
        load.start()

    barrier = pltpu.get_barrier_semaphore()
    for k in range(1, n):
        pl.semaphore_signal(
            barrier,
            inc=1,
            device_id={"tensor": lax.rem(t + k, n)},
            device_id_type=pl.DeviceIdType.MESH,
        )
    pl.semaphore_wait(barrier, n - 1)

    def remote(src, dst, send_sem, recv_sem, device):
        return pltpu.make_async_remote_copy(
            src_ref=src,
            dst_ref=dst,
            send_sem=send_sem,
            recv_sem=recv_sem,
            device_id={"tensor": device},
            device_id_type=pl.DeviceIdType.MESH,
        )

    def shrink_copy(k, sender, device):
        return remote(
            s_hbm.at[:, :, heads_columns(device)], s_all.at[sender], s_send.at[k], s_recv.at[k], device
        )

    def weight_copy(k, sender_j, jj):
        return remote(
            w_hbm.at[:, columns(jj)], w_all.at[sender_j], w_send.at[k], w_recv.at[k], first + jj
        )

    def expand_copy(k, sender_j, jj):
        return remote(
            e_hbm.at[:, columns(jj)], e_all.at[sender_j], e_send.at[k], e_recv.at[k], first + jj
        )

    for k in range(1, n):
        shrink_copy(k, t, lax.rem(t + k, n)).start()
    for k in range(1, SUB):
        weight_copy(k, j, lax.rem(j + k, SUB)).start()
    for k in range(1, SUB):
        expand_copy(k, j, lax.rem(j + k, SUB)).start()

    token_bounds, cache_bounds, adapter_rows = [jnp.int32(0)], [jnp.int32(0)], []
    for r in range(requests):
        token_bounds.append(token_bounds[r] + block_len[r])
        cache_bounds.append(cache_bounds[r] + cache_len[r])
        adapter_rows.append(storage_row[req_adapter[r]])

    lane1 = lax.broadcasted_iota(jnp.int32, (1, HD), 1)
    token_lo = jnp.zeros((1, HD), jnp.int32)
    token_hi = jnp.zeros((1, HD), jnp.int32)
    cache_lo = jnp.zeros((1, HD), jnp.int32)
    cache_hi = jnp.zeros((1, HD), jnp.int32)
    for r in range(requests):
        token_lo = jnp.where(lane1 == r, token_bounds[r], token_lo)
        token_hi = jnp.where(lane1 == r, token_bounds[r + 1], token_hi)
        cache_lo = jnp.where(lane1 == r, cache_bounds[r], cache_lo)
        cache_hi = jnp.where(lane1 == r, cache_bounds[r + 1], cache_hi)
    token_pos = lax.broadcasted_iota(jnp.int32, (tokens, HD), 0)
    token_in = (token_pos >= token_lo) & (token_pos < token_hi)
    q2[:, HD:] = jnp.where(token_in, 0.0, -BIG).astype(BF16)
    k2[0:tokens, HD:] = jnp.where(token_in, 1.0, 0.0).astype(BF16)
    ones = jnp.ones((tokens, HD), BF16)
    v2[0:tokens, HD:] = ones

    def augment(i, carry):
        at = pl.multiple_of(tokens + i * tokens, tokens)
        pos = token_pos + i * tokens
        inside = (pos >= cache_lo) & (pos < cache_hi)
        k2[pl.ds(at, tokens), HD:] = jnp.where(inside, 1.0, 0.0).astype(BF16)
        v2[pl.ds(at, tokens), HD:] = ones
        return carry

    lax.fori_loop(0, cached // tokens, augment, 0)
    for load in loads:
        load.wait()
    for load in own_loads:
        load.wait()

    scale = HD**-0.5 * math.log2(math.e)
    adapters = n * own_adapters

    def att_copy(c, k, sender_j, jj):
        span = pl.ds(c * q_chunk, q_chunk)
        return remote(
            att_all.at[sender_j, span],
            att_all.at[sender_j, span],
            a_send.at[c, k],
            a_recv.at[c, k],
            first + jj,
        )

    def row_slice(ref, device):
        return ref.at[pl.ds(pl.multiple_of(device * rows, rows), rows)]

    def shr_copy(sender, device):
        return remote(
            row_slice(shr_part, device),
            shr_recv.at[sender],
            p_send.at[device],
            p_recv.at[sender],
            device,
        )

    for c in range(chunks):
        q = q2[pl.ds(c * q_chunk, q_chunk), :]
        scores = dot_nt(q, k2[0:tokens, :])
        row = lax.broadcasted_iota(jnp.int32, scores.shape, 0) + c * q_chunk
        col = lax.broadcasted_iota(jnp.int32, scores.shape, 1)
        scores = jnp.where(col <= row, scores, -BIG)
        top = jnp.max(scores, axis=1, keepdims=True)
        p = jnp.exp2((scores - top) * scale).astype(BF16)
        acc = jnp.dot(p, v2[0:tokens, :], preferred_element_type=F32)

        def step(i, carry):
            top, acc = carry
            at = pl.multiple_of(tokens + i * key_block, 512)
            scores = dot_nt(q, k2[pl.ds(at, key_block), :])
            new_top = jnp.maximum(top, jnp.max(scores, axis=1, keepdims=True))
            p = jnp.exp2((scores - new_top) * scale).astype(BF16)
            acc = acc * jnp.exp2((top - new_top) * scale)
            return new_top, acc + jnp.dot(p, v2[pl.ds(at, key_block), :], preferred_element_type=F32)

        top, acc = lax.fori_loop(0, cached // key_block, step, (top, acc))
        attended = (acc[:, :HD] / acc[:, HD:]).astype(BF16)
        span = pl.ds(c * q_chunk, q_chunk)
        att_all[j, span] = attended
        for k in range(1, SUB):
            att_copy(c, k, j, lax.rem(j + k, SUB)).start()

        if c == 0:
            for k in range(1, n):
                shrink_copy(k, lax.rem(t + n - k, n), t).wait_recv()
        pos = lax.broadcasted_iota(jnp.int32, (q_chunk, HD), 0) + c * q_chunk
        lane = lax.broadcasted_iota(jnp.int32, (q_chunk, HD), 1)
        token_row = pick(pos, token_bounds, adapter_rows, jnp.zeros((q_chunk, HD), jnp.int32))
        half = jnp.where(lane >= HD // 2, 1, 0)
        shr = jnp.zeros((q_chunk, HD), F32)
        for a in range(0, adapters, 2):
            matrices = s_all[a // own_adapters].reshape(HD, HD)
            product = dot_nt(attended, matrices)
            shr = jnp.where(token_row == half + a, product, shr)
        shr_part[span, :] = pack(shr + pltpu.roll(shr, HD // 2, 1), shr_part.dtype)
        for k in range(per_chunk):
            device = c * per_chunk + lax.rem(t + k, per_chunk)

            @pl.when(device != t)
            def _():
                shr_copy(t, device).start()

    total = unpack(row_slice(shr_part, t)[...])
    for k in range(1, n):
        sender = lax.rem(t + n - k, n)
        shr_copy_in = remote(
            row_slice(shr_part, t), shr_recv.at[sender], p_send.at[sender], p_recv.at[sender], sender
        )
        shr_copy_in.wait_recv()
        total = total + unpack(shr_recv[sender])
    row_slice(shr_full, t)[...] = pack(total, shr_full.dtype)

    def full_copy(k, sender, device):
        return remote(
            row_slice(shr_full, sender), row_slice(shr_full, sender), f_send.at[k], f_recv.at[k], device
        )

    for k in range(1, n):
        full_copy(k, t, lax.rem(t + k, n)).start()

    for k in range(1, SUB):
        source = lax.rem(j + SUB - k, SUB)
        weight_copy(k, source, j).wait_recv()
        for c in range(chunks):
            att_copy(c, k, source, j).wait_recv()
    for c in range(chunks):
        span = pl.ds(c * q_chunk, q_chunk)
        value = jnp.dot(att_all[0, span], w_all[0], preferred_element_type=F32)
        for s in range(1, SUB):
            value = value + jnp.dot(att_all[s, span], w_all[s], preferred_element_type=F32)
        base[span, :] = value

    for k in range(1, SUB):
        expand_copy(k, lax.rem(j + SUB - k, SUB), j).wait_recv()
    for k in range(1, n):
        full_copy(k, lax.rem(t + n - k, n), t).wait_recv()

    def part_copy(sender, device):
        return remote(part.at[device], recv.at[sender], o_send.at[device], o_recv.at[sender], device)

    for c in range(chunks):
        span = pl.ds(c * q_chunk, q_chunk)
        pos = lax.broadcasted_iota(jnp.int32, (q_chunk, HD), 0) + c * q_chunk
        lane = lax.broadcasted_iota(jnp.int32, (q_chunk, HD), 1)
        token_row = pick(pos, token_bounds, adapter_rows, jnp.zeros((q_chunk, HD), jnp.int32))
        half = jnp.where(lane >= HD // 2, 1, 0)
        shrunk = unpack(shr_full[span, :])
        value = base[span, :]
        for s in range(SUB):
            mine = jnp.where(token_row == half + (first + s) * own_adapters, shrunk, 0.0)
            high = mine.astype(BF16)
            low = (mine - high.astype(F32)).astype(BF16)
            value = value + jnp.dot(high, e_all[s], preferred_element_type=F32)
            value = value + jnp.dot(low, e_all[s], preferred_element_type=F32)
        per = value.astype(part.dtype).reshape(per_chunk, rows, width)
        part[pl.ds(c * per_chunk, per_chunk)] = per
        for k in range(per_chunk):
            device = c * per_chunk + lax.rem(t + k, per_chunk)

            @pl.when(device != t)
            def _():
                part_copy(t, device).start()

    recv[t] = part[t]
    for k in range(1, n):
        sender = lax.rem(t + n - k, n)
        part_in = remote(part.at[sender], recv.at[sender], o_send.at[sender], o_recv.at[sender], sender)
        part_in.wait_recv()
    for s in range(SUB):
        value = recv[s].astype(F32)
        for z in range(1, n // SUB):
            value = value + recv[z * SUB + s].astype(F32)
        out_ref[:, s * width : (s + 1) * width] = value.astype(out_ref.dtype)

    for k in range(1, n):
        device = lax.rem(t + k, n)
        shrink_copy(k, t, device).wait_send()
        full_copy(k, t, device).wait_send()
        shr_copy(t, device).wait_send()
        part_copy(t, device).wait_send()
    for k in range(1, SUB):
        jj = lax.rem(j + k, SUB)
        weight_copy(k, j, jj).wait_send()
        expand_copy(k, j, jj).wait_send()
        for c in range(chunks):
            att_copy(c, k, j, jj).wait_send()


def on_device(
    queries,
    block_key_rows,
    block_value_rows,
    cached_key_rows,
    cached_value_rows,
    output_projection_weight,
    stored_shrink_matrices,
    stored_expand_matrices,
    request_adapter_index,
    adapter_storage_row,
    block_token_lengths,
    cached_token_lengths,
):
    n = lax.axis_size("tensor")
    tokens = queries.shape[0]
    cached = cached_key_rows.shape[0]
    model = output_projection_weight.shape[1]
    own, _, rank = stored_shrink_matrices.shape
    rows = tokens // n
    width = model // SUB
    q_chunk = 256
    key_block = 1536
    chunks = tokens // q_chunk
    send_type = BF16 if rows % 16 == 0 else F32
    shrink_t = stored_shrink_matrices.transpose(0, 2, 1)
    expand = stored_expand_matrices.reshape(own * rank, model)
    hbm = pl.BlockSpec(memory_space=pl.ANY)
    smem = pl.BlockSpec(memory_space=pltpu.SMEM)
    dma = pltpu.SemaphoreType.DMA
    return pl.pallas_call(
        functools.partial(kernel, n, q_chunk, key_block),
        out_shape=jax.ShapeDtypeStruct((rows, model), BF16),
        in_specs=[hbm] * 8 + [smem] * 4,
        out_specs=pl.BlockSpec(memory_space=pltpu.VMEM),
        scratch_shapes=[
            pltpu.VMEM((tokens, 2 * HD), BF16),
            pltpu.VMEM((tokens + cached, 2 * HD), BF16),
            pltpu.VMEM((tokens + cached, 2 * HD), BF16),
            pltpu.VMEM((SUB, HD, width), BF16),
            pltpu.VMEM((SUB, own * rank, width), BF16),
            pltpu.VMEM((n, own, rank, HD), BF16),
            pltpu.VMEM((SUB, tokens, HD), BF16),
            pltpu.VMEM((tokens, HD), send_type),
            pltpu.VMEM((n, rows, HD), send_type),
            pltpu.VMEM((tokens, HD), send_type),
            pltpu.VMEM((n, rows, width), send_type),
            pltpu.VMEM((n, rows, width), send_type),
            pltpu.VMEM((tokens, width), F32),
            dma((8,)),
            dma((SUB,)),
            dma((SUB,)),
            dma((SUB,)),
            dma((SUB,)),
            dma((n,)),
            dma((n,)),
            dma((chunks, SUB)),
            dma((chunks, SUB)),
            dma((n,)),
            dma((n,)),
            dma((n,)),
            dma((n,)),
            dma((n,)),
            dma((n,)),
        ],
        compiler_params=pltpu.CompilerParams(
            collective_id=0, has_side_effects=True, vmem_limit_bytes=56 * 1024 * 1024
        ),
    )(
        queries,
        block_key_rows,
        block_value_rows,
        cached_key_rows,
        cached_value_rows,
        output_projection_weight,
        shrink_t,
        expand,
        request_adapter_index,
        adapter_storage_row,
        block_token_lengths,
        cached_token_lengths,
    )


def solution(mesh):
    placed = (
        P("groups", "tensor"),
        P("groups", "tensor"),
        P("groups", "tensor"),
        P("groups", "tensor"),
        P("groups", "tensor"),
        P("tensor", None),
        P("tensor", None, None),
        P("tensor", None, None),
        P("groups"),
        P(),
        P("groups"),
        P("groups"),
    )
    return jax.shard_map(
        on_device,
        mesh=mesh,
        in_specs=placed,
        out_specs=P(("groups", "tensor"), None),
        check_vma=False,
    )
```

```python
import functools
import math

import jax
import jax.numpy as jnp
from jax import lax
from jax.experimental import pallas as pl
from jax.experimental.pallas import tpu as pltpu
from jax.sharding import PartitionSpec as P

HD = 128
SUB = 8
BIG = 2.0**40
F32 = jnp.float32
BF16 = jnp.bfloat16


def dot_nt(a, b):
    return lax.dot_general(a, b, (((1,), (1,)), ((), ())), preferred_element_type=F32)


def pick(position, bounds, values, like):
    out = like
    for r, value in enumerate(values):
        inside = (position >= bounds[r]) & (position < bounds[r + 1])
        out = jnp.where(inside, value, out)
    return out


def pack(twice, kind):
    high = twice.astype(BF16).astype(F32)
    lane = lax.broadcasted_iota(jnp.int32, twice.shape, 1)
    return jnp.where(lane < HD // 2, high, twice - high).astype(kind)


def unpack(packed):
    halves = packed.astype(F32)
    return halves + pltpu.roll(halves, HD // 2, 1)


def kernel(
    n,
    q_chunk,
    key_block,
    q_hbm,
    bk_hbm,
    bv_hbm,
    ck_hbm,
    cv_hbm,
    w_hbm,
    s_hbm,
    e_hbm,
    req_adapter,
    storage_row,
    block_len,
    cache_len,
    out_ref,
    q2,
    k2,
    v2,
    w_all,
    e_all,
    s_all,
    att_all,
    shr_part,
    shr_recv,
    shr_full,
    part,
    recv,
    load_sem,
    w_send,
    w_recv,
    e_send,
    e_recv,
    s_send,
    s_recv,
    a_send,
    a_recv,
    p_send,
    p_recv,
    f_send,
    f_recv,
    o_send,
    o_recv,
    x_send,
    x_recv,
):
    t = lax.axis_index("tensor")
    j = lax.rem(t, SUB)
    first = t - j
    group = lax.axis_index("groups")
    shared = lax.axis_size("groups") % 2 == 0
    side = lax.rem(group, 2)
    twin = group + 1 - 2 * side
    tokens = q_hbm.shape[0]
    cached = ck_hbm.shape[0]
    requests = block_len.shape[0]
    rows = tokens // n
    width = w_hbm.shape[1] // SUB
    own_adapters = s_hbm.shape[0]
    chunks = tokens // q_chunk
    per_chunk = n // chunks

    loads = [
        pltpu.make_async_copy(q_hbm, q2.at[:, pl.ds(0, HD)], load_sem.at[0]),
        pltpu.make_async_copy(bk_hbm, k2.at[pl.ds(0, tokens), pl.ds(0, HD)], load_sem.at[1]),
        pltpu.make_async_copy(ck_hbm, k2.at[pl.ds(tokens, cached), pl.ds(0, HD)], load_sem.at[2]),
        pltpu.make_async_copy(bv_hbm, v2.at[pl.ds(0, tokens), pl.ds(0, HD)], load_sem.at[3]),
        pltpu.make_async_copy(cv_hbm, v2.at[pl.ds(tokens, cached), pl.ds(0, HD)], load_sem.at[4]),
    ]
    for load in loads:
        load.start()

    def columns(block):
        return pl.ds(pl.multiple_of(block * width, 128), width)

    def heads_columns(device):
        return pl.ds(pl.multiple_of(device * HD, HD), HD)

    own_loads = [
        pltpu.make_async_copy(w_hbm.at[:, columns(j)], w_all.at[j], load_sem.at[5]),
        pltpu.make_async_copy(e_hbm.at[:, columns(j)], e_all.at[j], load_sem.at[6]),
        pltpu.make_async_copy(s_hbm.at[:, :, heads_columns(t)], s_all.at[t], load_sem.at[7]),
    ]
    for load in own_loads:
        load.start()

    barrier = pltpu.get_barrier_semaphore()
    for k in range(1, n):
        pl.semaphore_signal(
            barrier,
            inc=1,
            device_id={"tensor": lax.rem(t + k, n)},
            device_id_type=pl.DeviceIdType.MESH,
        )
    if shared:
        pl.semaphore_signal(
            barrier,
            inc=1,
            device_id={"groups": twin, "tensor": t},
            device_id_type=pl.DeviceIdType.MESH,
        )
    pl.semaphore_wait(barrier, n if shared else n - 1)

    def remote(src, dst, send_sem, recv_sem, device):
        return pltpu.make_async_remote_copy(
            src_ref=src,
            dst_ref=dst,
            send_sem=send_sem,
            recv_sem=recv_sem,
            device_id={"tensor": device},
            device_id_type=pl.DeviceIdType.MESH,
        )

    def shrink_copy(k, sender, device):
        return remote(
            s_hbm.at[:, :, heads_columns(device)], s_all.at[sender], s_send.at[k], s_recv.at[k], device
        )

    lines = HD // 2 if shared else HD
    own_lines = pl.ds(pl.multiple_of(side * lines, lines), lines) if shared else pl.ds(0, HD)
    twin_lines = pl.ds(pl.multiple_of((1 - side) * lines, lines), lines)

    def weight_copy(k, sender_j, jj):
        return remote(
            w_hbm.at[own_lines, columns(jj)],
            w_all.at[sender_j, own_lines],
            w_send.at[k],
            w_recv.at[k],
            first + jj,
        )

    def twin_copy(k, sender_j, span):
        return pltpu.make_async_remote_copy(
            src_ref=w_all.at[sender_j, span],
            dst_ref=w_all.at[sender_j, span],
            send_sem=x_send.at[k],
            recv_sem=x_recv.at[k],
            device_id={"groups": twin, "tensor": t},
            device_id_type=pl.DeviceIdType.MESH,
        )

    def expand_copy(k, sender_j, jj):
        return remote(
            e_hbm.at[:, columns(jj)], e_all.at[sender_j], e_send.at[k], e_recv.at[k], first + jj
        )

    for k in range(1, n):
        shrink_copy(k, t, lax.rem(t + k, n)).start()
    for k in range(1, SUB):
        weight_copy(k, j, lax.rem(j + k, SUB)).start()
    for k in range(1, SUB):
        expand_copy(k, j, lax.rem(j + k, SUB)).start()

    token_bounds, cache_bounds, adapter_rows = [jnp.int32(0)], [jnp.int32(0)], []
    for r in range(requests):
        token_bounds.append(token_bounds[r] + block_len[r])
        cache_bounds.append(cache_bounds[r] + cache_len[r])
        adapter_rows.append(storage_row[req_adapter[r]])

    lane1 = lax.broadcasted_iota(jnp.int32, (1, HD), 1)
    token_lo = jnp.zeros((1, HD), jnp.int32)
    token_hi = jnp.zeros((1, HD), jnp.int32)
    cache_lo = jnp.zeros((1, HD), jnp.int32)
    cache_hi = jnp.zeros((1, HD), jnp.int32)
    for r in range(requests):
        token_lo = jnp.where(lane1 == r, token_bounds[r], token_lo)
        token_hi = jnp.where(lane1 == r, token_bounds[r + 1], token_hi)
        cache_lo = jnp.where(lane1 == r, cache_bounds[r], cache_lo)
        cache_hi = jnp.where(lane1 == r, cache_bounds[r + 1], cache_hi)
    token_pos = lax.broadcasted_iota(jnp.int32, (tokens, HD), 0)
    token_in = (token_pos >= token_lo) & (token_pos < token_hi)
    q2[:, HD:] = jnp.where(token_in, 0.0, -BIG).astype(BF16)
    k2[0:tokens, HD:] = jnp.where(token_in, 1.0, 0.0).astype(BF16)
    ones = jnp.ones((tokens, HD), BF16)
    v2[0:tokens, HD:] = ones

    def augment(i, carry):
        at = pl.multiple_of(tokens + i * tokens, tokens)
        pos = token_pos + i * tokens
        inside = (pos >= cache_lo) & (pos < cache_hi)
        k2[pl.ds(at, tokens), HD:] = jnp.where(inside, 1.0, 0.0).astype(BF16)
        v2[pl.ds(at, tokens), HD:] = ones
        return carry

    lax.fori_loop(0, cached // tokens, augment, 0)
    for load in loads:
        load.wait()
    for load in own_loads:
        load.wait()

    scale = HD**-0.5 * math.log2(math.e)
    adapters = n * own_adapters

    def att_copy(c, k, sender_j, jj):
        span = pl.ds(c * q_chunk, q_chunk)
        return remote(
            att_all.at[sender_j, span],
            att_all.at[sender_j, span],
            a_send.at[c, k],
            a_recv.at[c, k],
            first + jj,
        )

    def row_slice(ref, device):
        return ref.at[pl.ds(pl.multiple_of(device * rows, rows), rows)]

    def shr_copy(sender, device):
        return remote(
            row_slice(shr_part, device),
            shr_recv.at[sender],
            p_send.at[device],
            p_recv.at[sender],
            device,
        )

    def attend(c):
        q = q2[pl.ds(c * q_chunk, q_chunk), :]
        scores = dot_nt(q, k2[0:tokens, :])
        row = lax.broadcasted_iota(jnp.int32, scores.shape, 0) + c * q_chunk
        col = lax.broadcasted_iota(jnp.int32, scores.shape, 1)
        scores = jnp.where(col <= row, scores, -BIG)
        top = jnp.max(scores, axis=1, keepdims=True)
        p = jnp.exp2((scores - top) * scale).astype(BF16)
        acc = jnp.dot(p, v2[0:tokens, :], preferred_element_type=F32)

        def step(i, carry):
            top, acc = carry
            at = pl.multiple_of(tokens + i * key_block, 512)
            scores = dot_nt(q, k2[pl.ds(at, key_block), :])
            new_top = jnp.maximum(top, jnp.max(scores, axis=1, keepdims=True))
            p = jnp.exp2((scores - new_top) * scale).astype(BF16)
            acc = acc * jnp.exp2((top - new_top) * scale)
            return new_top, acc + jnp.dot(p, v2[pl.ds(at, key_block), :], preferred_element_type=F32)

        top, acc = lax.fori_loop(0, cached // key_block, step, (top, acc), unroll=2)
        attended = (acc[:, :HD] / acc[:, HD:]).astype(BF16)
        span = pl.ds(c * q_chunk, q_chunk)
        att_all[j, span] = attended
        for k in range(1, SUB):
            att_copy(c, k, j, lax.rem(j + k, SUB)).start()

        if c == 0:
            for k in range(1, n):
                shrink_copy(k, lax.rem(t + n - k, n), t).wait_recv()
            for k in range(1, SUB):
                source = lax.rem(j + SUB - k, SUB)
                weight_copy(k, source, j).wait_recv()
                if shared:
                    twin_copy(k, source, own_lines).start()
        pos = lax.broadcasted_iota(jnp.int32, (q_chunk, HD), 0) + c * q_chunk
        lane = lax.broadcasted_iota(jnp.int32, (q_chunk, HD), 1)
        token_row = pick(pos, token_bounds, adapter_rows, jnp.zeros((q_chunk, HD), jnp.int32))
        half = jnp.where(lane >= HD // 2, 1, 0)
        shr = jnp.zeros((q_chunk, HD), F32)
        for a in range(0, adapters, 2):
            matrices = s_all[a // own_adapters].reshape(HD, HD)
            product = dot_nt(attended, matrices)
            shr = jnp.where(token_row == half + a, product, shr)
        shr_part[span, :] = pack(shr + pltpu.roll(shr, HD // 2, 1), shr_part.dtype)
        for k in range(per_chunk):
            device = c * per_chunk + lax.rem(t + k, per_chunk)

            @pl.when(device != t)
            def _():
                shr_copy(t, device).start()

    def full_copy(sender, device):
        return remote(
            row_slice(shr_full, sender),
            row_slice(shr_full, sender),
            f_send.at[device],
            f_recv.at[sender],
            device,
        )

    def collect(c):
        @pl.when(t // per_chunk == c)
        def _():
            total = unpack(row_slice(shr_part, t)[...])
            for k in range(1, n):
                sender = lax.rem(t + n - k, n)
                shr_copy_in = remote(
                    row_slice(shr_part, t), shr_recv.at[sender], p_send.at[sender], p_recv.at[sender], sender
                )
                shr_copy_in.wait_recv()
                total = total + unpack(shr_recv[sender])
            row_slice(shr_full, t)[...] = pack(total, shr_full.dtype)
            for k in range(1, n):
                full_copy(t, lax.rem(t + k, n)).start()

    def part_copy(sender, device):
        return remote(part.at[device], recv.at[sender], o_send.at[device], o_recv.at[sender], device)

    def project(c):
        for k in range(1, SUB):
            source = lax.rem(j + SUB - k, SUB)
            att_copy(c, k, source, j).wait_recv()
            if c == 0:
                if shared:
                    twin_copy(k, source, twin_lines).wait_recv()
                expand_copy(k, source, j).wait_recv()
        for k in range(per_chunk):
            owner = c * per_chunk + lax.rem(t + k, per_chunk)

            @pl.when(owner != t)
            def _():
                full_copy(owner, t).wait_recv()

        span = pl.ds(c * q_chunk, q_chunk)
        value = jnp.dot(att_all[0, span], w_all[0], preferred_element_type=F32)
        for s in range(1, SUB):
            value = value + jnp.dot(att_all[s, span], w_all[s], preferred_element_type=F32)
        pos = lax.broadcasted_iota(jnp.int32, (q_chunk, HD), 0) + c * q_chunk
        lane = lax.broadcasted_iota(jnp.int32, (q_chunk, HD), 1)
        token_row = pick(pos, token_bounds, adapter_rows, jnp.zeros((q_chunk, HD), jnp.int32))
        half = jnp.where(lane >= HD // 2, 1, 0)
        shrunk = unpack(shr_full[span, :])
        for s in range(SUB):
            mine = jnp.where(token_row == half + (first + s) * own_adapters, shrunk, 0.0)
            high = mine.astype(BF16)
            low = (mine - high.astype(F32)).astype(BF16)
            value = value + jnp.dot(high, e_all[s], preferred_element_type=F32)
            value = value + jnp.dot(low, e_all[s], preferred_element_type=F32)
        per = value.astype(part.dtype).reshape(per_chunk, rows, width)
        part[pl.ds(c * per_chunk, per_chunk)] = per
        for k in range(per_chunk):
            device = c * per_chunk + lax.rem(t + k, per_chunk)

            @pl.when(device != t)
            def _():
                part_copy(t, device).start()

    for c in range(chunks):
        attend(c)
        if c > 0:
            collect(c - 1)
    project(0)
    collect(chunks - 1)
    for c in range(1, chunks):
        project(c)

    recv[t] = part[t]
    for k in range(1, n):
        sender = lax.rem(t + n - k, n)
        part_in = remote(part.at[sender], recv.at[sender], o_send.at[sender], o_recv.at[sender], sender)
        part_in.wait_recv()
    for s in range(SUB):
        value = recv[s].astype(F32)
        for z in range(1, n // SUB):
            value = value + recv[z * SUB + s].astype(F32)
        out_ref[:, s * width : (s + 1) * width] = value.astype(out_ref.dtype)

    for k in range(1, n):
        device = lax.rem(t + k, n)
        shrink_copy(k, t, device).wait_send()
        full_copy(t, device).wait_send()
        shr_copy(t, device).wait_send()
        part_copy(t, device).wait_send()
    for k in range(1, SUB):
        jj = lax.rem(j + k, SUB)
        weight_copy(k, j, jj).wait_send()
        if shared:
            twin_copy(k, jj, own_lines).wait_send()
        expand_copy(k, j, jj).wait_send()
        for c in range(chunks):
            att_copy(c, k, j, jj).wait_send()


def on_device(
    queries,
    block_key_rows,
    block_value_rows,
    cached_key_rows,
    cached_value_rows,
    output_projection_weight,
    stored_shrink_matrices,
    stored_expand_matrices,
    request_adapter_index,
    adapter_storage_row,
    block_token_lengths,
    cached_token_lengths,
):
    n = lax.axis_size("tensor")
    tokens = queries.shape[0]
    cached = cached_key_rows.shape[0]
    model = output_projection_weight.shape[1]
    own, _, rank = stored_shrink_matrices.shape
    rows = tokens // n
    width = model // SUB
    q_chunk = 128
    key_block = 3072
    chunks = tokens // q_chunk
    send_type = BF16 if rows % 16 == 0 else F32
    shrink_t = stored_shrink_matrices.transpose(0, 2, 1)
    expand = stored_expand_matrices.reshape(own * rank, model)
    hbm = pl.BlockSpec(memory_space=pl.ANY)
    smem = pl.BlockSpec(memory_space=pltpu.SMEM)
    dma = pltpu.SemaphoreType.DMA
    return pl.pallas_call(
        functools.partial(kernel, n, q_chunk, key_block),
        out_shape=jax.ShapeDtypeStruct((rows, model), BF16),
        in_specs=[hbm] * 8 + [smem] * 4,
        out_specs=pl.BlockSpec(memory_space=pltpu.VMEM),
        scratch_shapes=[
            pltpu.VMEM((tokens, 2 * HD), BF16),
            pltpu.VMEM((tokens + cached, 2 * HD), BF16),
            pltpu.VMEM((tokens + cached, 2 * HD), BF16),
            pltpu.VMEM((SUB, HD, width), BF16),
            pltpu.VMEM((SUB, own * rank, width), BF16),
            pltpu.VMEM((n, own, rank, HD), BF16),
            pltpu.VMEM((SUB, tokens, HD), BF16),
            pltpu.VMEM((tokens, HD), send_type),
            pltpu.VMEM((n, rows, HD), send_type),
            pltpu.VMEM((tokens, HD), send_type),
            pltpu.VMEM((n, rows, width), send_type),
            pltpu.VMEM((n, rows, width), send_type),
            dma((8,)),
            dma((SUB,)),
            dma((SUB,)),
            dma((SUB,)),
            dma((SUB,)),
            dma((n,)),
            dma((n,)),
            dma((chunks, SUB)),
            dma((chunks, SUB)),
            dma((n,)),
            dma((n,)),
            dma((n,)),
            dma((n,)),
            dma((n,)),
            dma((n,)),
            dma((SUB,)),
            dma((SUB,)),
        ],
        compiler_params=pltpu.CompilerParams(
            collective_id=0, has_side_effects=True, vmem_limit_bytes=56 * 1024 * 1024
        ),
    )(
        queries,
        block_key_rows,
        block_value_rows,
        cached_key_rows,
        cached_value_rows,
        output_projection_weight,
        shrink_t,
        expand,
        request_adapter_index,
        adapter_storage_row,
        block_token_lengths,
        cached_token_lengths,
    )


def solution(mesh):
    placed = (
        P("groups", "tensor"),
        P("groups", "tensor"),
        P("groups", "tensor"),
        P("groups", "tensor"),
        P("groups", "tensor"),
        P("tensor", None),
        P("tensor", None, None),
        P("tensor", None, None),
        P("groups"),
        P(),
        P("groups"),
        P("groups"),
    )
    return jax.shard_map(
        on_device,
        mesh=mesh,
        in_specs=placed,
        out_specs=P(("groups", "tensor"), None),
        check_vma=False,
    )
```
